128 devices in a mesh: row: 8 (over z, y_hi), col: 16 (over x, y_lo, core).
Axes of the slice: x: 4, y: 4 (y_hi: 2, y_lo: 2; y = y_hi * 2 + y_lo), z: 4, core: 2. Of those that a mesh axis runs over, the one named last changes fastest.
Arguments:
- val_wave: bfloat16 [8, 64, 64, 128], replicated, may hold values from -6 to 6
- cond_wave: bfloat16 [128, 64, 64, 128], P(('row', 'col')), may hold values from -6 to 6
- val_energy: float32 [8], replicated, may hold values from -12 to -0.5
- cond_energy: float32 [128], replicated, may hold values from 0.5 to 20
- band_owner: int32 [128], P(('row', 'col')), may hold values from 0 to 127, each once
- grid_map: int32 [30720], replicated, may hold values from 0 to 262143, as said below
Outputs:
- chi: float32 [2, 2048, 30720], P(None, 'row', 'col')
The draws below stay inside these ranges and needn't reach their ends.
Inputs may be any that keep to these rules, and one draw needn't show every extreme that they name: `band_owner`: every one of the 128 band numbers stands in exactly one slot. `grid_map`: 30720 distinct flat grid points: those of the shortest wave vectors, with indices above 32 read as negative frequencies, ordered by length with ties in random order.
All inputs are finite; a program needn't handle non-finite values.
Results may differ from the reference program's by a relative error of at most 0.0041.
Values may be sent and summed in bfloat16 or wider, within the bound.
A program may use at most 576 MiB of HBM per device.

```python
import jax
import jax.numpy as jnp
from jax import lax

GRID = 64
NG = 30720
NV = 8
NC = 128
PAIRS = 1024
SLAB = 2048


def signed_freq(index):
    return jnp.where(index < GRID // 2, index, index - GRID)


def draw_grid_map(key, part):
    points = jnp.arange(GRID * GRID * GRID, dtype=jnp.int32)
    first = signed_freq(points // (GRID * GRID))
    second = signed_freq(points // GRID % GRID)
    third = signed_freq(points % GRID)
    length = first * first + second * second + third * third
    shuffle = jax.random.permutation(key, GRID * GRID * GRID).astype(jnp.int32)
    scores = length * (GRID * GRID * GRID) + shuffle
    ranked, chosen = lax.top_k(-scores, NG)
    return chosen.astype(jnp.int32)


def shard_levels(rng, shape, shards, least, top_value):
    factor_of, own = 1.0, jax.random.fold_in(rng, 6)
    for dim, blocks in shards:
        steps = jnp.exp(jax.random.uniform(jax.random.fold_in(own, dim), (blocks,), jnp.float32, least / len(shards), top_value / len(shards)))
        factor_of = factor_of * jnp.repeat(steps, shape[dim] // blocks).reshape([-1 if axis == dim else 1 for axis in range(len(shape))])
    return factor_of


def centred(stream_key, shape, width, limit, shards=(), held_as=jnp.bfloat16):
    drawn = jax.random.normal(stream_key, shape, jnp.float32) * width
    if len(shards) > 0:
        drawn = shard_levels(stream_key, shape, shards, -0.22, 0.18) * drawn
    return jnp.clip(drawn, min=-limit, max=limit).astype(held_as)


def setup_inputs(seed: int = 0) -> dict:
    streams_of = jax.random.split(jax.random.key(seed), 7)
    val_wave = centred(streams_of[0], (NV, GRID, GRID, 2 * GRID), 1.0, 6.0)
    cond_wave = centred(streams_of[1], (NC, GRID, GRID, 2 * GRID), 1.0, 6.0, ((0, 128),))
    val_energy = jnp.clip(jax.random.uniform(streams_of[2], (NV,), jnp.float32, -12.0, -0.5), -12.0, -0.5)
    cond_energy = jnp.clip(jax.random.uniform(streams_of[3], (NC,), jnp.float32, 0.5, 20.0), 0.5, 20.0)
    band_owner = jax.random.permutation(streams_of[4], NC).astype(jnp.int32)
    grid_map = draw_grid_map(jax.random.fold_in(streams_of[6], 71), 0)
    return dict(val_wave=val_wave, cond_wave=cond_wave, val_energy=val_energy, cond_energy=cond_energy, band_owner=band_owner, grid_map=grid_map)


def reference(val_wave, cond_wave, val_energy, cond_energy, band_owner, grid_map):
    valence = val_wave.astype(jnp.float32)
    valence_re = valence[..., :GRID]
    valence_im = valence[..., GRID:]
    band_numbers = jnp.arange(NC, dtype=jnp.int32)
    scaling = 1.0 / float(GRID) ** 1.5

    def one_band(operands):
        wave, number = operands
        conduction = wave.astype(jnp.float32)
        conduction_re = conduction[..., :GRID]
        conduction_im = conduction[..., GRID:]
        dens_re = valence_re * conduction_re[None] + valence_im * conduction_im[None]
        dens_im = valence_re * conduction_im[None] - valence_im * conduction_re[None]
        spectrum = jnp.fft.fftn(lax.complex(dens_re, dens_im), axes=(1, 2, 3))
        picked = spectrum.reshape(NV, GRID * GRID * GRID)[:, grid_map]
        pair_dens = jnp.stack([jnp.real(picked) * scaling, jnp.imag(picked) * scaling])
        energy = jnp.sum(jnp.where(number == band_numbers, cond_energy, 0.0))
        weight = -2.0 / (PAIRS ** 0.5 * (energy - val_energy))
        weighted = (weight[None, :, None] * pair_dens[:, :, :SLAB]).astype(jnp.bfloat16)
        plain = pair_dens.astype(jnp.bfloat16)
        return weighted, plain

    weighted, plain = lax.map(one_band, (cond_wave, band_owner))
    weighted = weighted.transpose(1, 0, 2, 3).reshape(2, PAIRS, SLAB).astype(jnp.float32)
    plain = plain.transpose(1, 0, 2, 3).reshape(2, PAIRS, NG).astype(jnp.float32)
    left_re = jnp.concatenate([weighted[0], weighted[1]], 0)
    left_im = jnp.concatenate([weighted[1], -weighted[0]], 0)
    right = jnp.concatenate([plain[0], plain[1]], 0)
    chi_re = jnp.dot(left_re.T, right, precision=lax.Precision.HIGHEST, preferred_element_type=jnp.float32)
    chi_im = jnp.dot(left_im.T, right, precision=lax.Precision.HIGHEST, preferred_element_type=jnp.float32)
    return jnp.stack([chi_re, chi_im])
```

```python
import functools
import math

import jax
import jax.numpy as jnp
import ml_dtypes
import numpy as np
from jax import lax
from jax.experimental import pallas as pl
from jax.experimental.pallas import tpu as pltpu
from jax.sharding import PartitionSpec as P

GRID = 64
NG = 30720
SLAB = 2048
ROWS = 8
COLS = 16
G_COL = NG // COLS
G_ROW = SLAB // ROWS
MAGS = 20
CELLS = MAGS * MAGS
LANES = 128


def shells():
    points = np.arange(GRID)
    freq = np.where(points < GRID // 2, points, points - GRID)
    square = freq * freq
    length = (square[:, None, None] + square[None, :, None] + square[None, None, :]).ravel()
    length = np.sort(length, kind="stable")
    assert length[NG - 1] < MAGS * MAGS
    return length


def orbit_lists(width, count):
    length = shells()
    mags = np.arange(MAGS)
    a, b, c = np.meshgrid(mags, mags, mags, indexing="ij")
    a, b, c = a.ravel(), b.ravel(), c.ravel()
    square = a * a + b * b + c * c
    source = c * CELLS + (b // 4) * (4 * MAGS) + a * 4 + b % 4
    code = (a * GRID + b) * GRID + c
    lists = []
    for block in range(count):
        least, most = length[block * width], length[(block + 1) * width - 1]
        lists.append(np.nonzero((square >= least) & (square <= most))[0])
    rows = -(-max(len(picked) for picked in lists) // 16) * 16
    index = np.zeros((count, rows), np.int32)
    codes = np.full((count, 1, rows), -1, np.int32)
    for block, picked in enumerate(lists):
        index[block, : len(picked)] = source[picked]
        codes[block, 0, : len(picked)] = code[picked]
    return index, codes


def split_table(table):
    high = table.astype(ml_dtypes.bfloat16)
    low = (table - high.astype(np.float64)).astype(ml_dtypes.bfloat16)
    return np.concatenate([high, low], 0)


def dft_tables():
    point = np.arange(GRID)
    mag = np.arange(MAGS)
    angle = (mag[:, None] * point[None, :] % GRID) * (2.0 * math.pi / GRID)
    parts = np.stack([np.cos(angle), np.sin(angle)])
    table_b = np.zeros((2, MAGS // 4, 4, 4, 4, GRID))
    for a in range(4):
        table_b[:, :, a, :, a, :] = parts.reshape(2, MAGS // 4, 4, GRID)
    table_a = np.zeros((2, MAGS, 4, GRID, 4))
    for b in range(4):
        table_a[:, :, b, :, b] = parts
    table_c = np.zeros((MAGS, 2, 2, 2, 2, 2, GRID))
    for v in range(2):
        for sign in range(2):
            turn = 1.0 - 2.0 * sign
            table_c[:, v, 0, sign, 0, v] = parts[0]
            table_c[:, v, 0, sign, 1, v] = turn * parts[1]
            table_c[:, v, 1, sign, 1, v] = parts[0]
            table_c[:, v, 1, sign, 0, v] = -turn * parts[1]
    table_c = table_c * (1.0 / float(GRID) ** 1.5)
    return (
        split_table(table_b.reshape(8 * MAGS, 4 * GRID)),
        split_table(table_a.reshape(8 * MAGS, 4 * GRID)),
        split_table(table_c.reshape(8 * MAGS, 4 * GRID)),
    )


def dot_nn(left, right):
    return lax.dot_general(
        left, right, (((1,), (0,)), ((), ())), preferred_element_type=jnp.float32
    )


def dot_nt(left, right):
    return lax.dot_general(
        left, right, (((1,), (1,)), ((), ())), preferred_element_type=jnp.float32
    )


def halves(value):
    high = value.astype(jnp.bfloat16)
    return high, (value - high.astype(jnp.float32)).astype(jnp.bfloat16)


def three(dot, table, high, low):
    rows = table.shape[0] // 2
    both = dot(table, high)
    return both[:rows] + both[rows:] + dot(table[:rows], low)


def signs(both, rows):
    cos_re, cos_im = both[:rows, :LANES], both[:rows, LANES:]
    sin_re, sin_im = both[rows:, :LANES], both[rows:, LANES:]
    plus = jnp.concatenate([cos_re + sin_im, cos_im - sin_re], 1)
    minus = jnp.concatenate([cos_re - sin_im, cos_im + sin_re], 1)
    return plus, minus


def spectrum_kernel(
    owner, cond_energy, val_energy, index_p, index_w,
    val, cond, table_b, table_a, table_c,
    plain, weighted,
    zh, zl, uh, ul, sums, cells, picked,
):
    step = pl.program_id(0)
    block = 4 * GRID
    first = lax.broadcasted_iota(jnp.int32, (block, LANES), 1) < GRID
    tb = table_b[...]

    def along_b(t, carry):
        rows = pl.ds(t * 4, 4)
        slot = cond[0, rows].reshape(block, LANES).astype(jnp.float32)
        one = val[0, rows].reshape(block, LANES).astype(jnp.float32)
        two = val[1, rows].reshape(block, LANES).astype(jnp.float32)
        slot_t = pltpu.roll(slot, GRID, 1)
        one_t = pltpu.roll(one, GRID, 1)
        two_t = pltpu.roll(two, GRID, 1)
        slot_re = jnp.where(first, slot, slot_t)
        slot_im = jnp.where(first, slot_t, slot)
        val_re = jnp.where(first, one, two_t)
        val_im = jnp.where(first, one_t, two)
        dens_re = val_re * slot_re + val_im * slot_im
        dens_im = val_re * slot_im - val_im * slot_re
        high, low = halves(jnp.concatenate([dens_re, dens_im], 1))
        both = three(dot_nn, tb, high, low)
        out = pl.ds(pl.multiple_of(t * 16, 16), 16)
        for sign, value in enumerate(signs(both, 4 * MAGS)):
            high, low = halves(value)
            for group in range(MAGS // 4):
                zh[sign * 5 + group, out, :] = high[group * 16 : group * 16 + 16]
                zl[sign * 5 + group, out, :] = low[group * 16 : group * 16 + 16]
        return carry

    lax.fori_loop(0, GRID // 4, along_b, 0)
    ta = table_a[...]

    def along_a(group, carry):
        out = pl.ds(pl.multiple_of(group * 80, 16), 80)
        for sign_b in range(2):
            both = three(dot_nn, ta, zh[sign_b * 5 + group], zl[sign_b * 5 + group])
            for sign_a, value in enumerate(signs(both, 4 * MAGS)):
                high, low = halves(value)
                uh[sign_a * 2 + sign_b, out, :] = high
                ul[sign_a * 2 + sign_b, out, :] = low
        return carry

    lax.fori_loop(0, MAGS // 4, along_a, 0)
    tc = table_c[...]

    def along_c(pair, carry):
        value = three(dot_nt, tc, uh[pair], ul[pair])
        value = value.reshape(MAGS, 8, CELLS)
        sums[:, pl.ds(pl.multiple_of((pair * 4 + step) * 8, 8), 8), :CELLS] = value
        return carry

    lax.fori_loop(0, 4, along_c, 0)

    @pl.when(step == pl.num_programs(0) - 1)
    def _():
        def turn(mag, carry):
            value = jnp.transpose(sums[mag], (1, 0))
            cells[pl.ds(pl.multiple_of(mag * CELLS, 8), CELLS), :] = value[:CELLS]
            return carry

        lax.fori_loop(0, MAGS, turn, 0)
        lane = lax.broadcasted_iota(jnp.int32, (1, LANES), 1)
        band = (lane >> 3) % 4 * 2 + (lane >> 2) % 2
        gap = jnp.zeros((1, LANES), jnp.float32)
        energy = cond_energy[owner[0]]
        for v in range(8):
            gap = jnp.where(band == v, energy - val_energy[v], gap)
        weight = -2.0 / (math.sqrt(8 * LANES) * gap)
        rows = index_p.shape[1]

        def slab(block, carry):
            def row(i, inner):
                for k in range(16):
                    picked[pl.ds(i * 16 + k, 1), :] = cells[pl.ds(index_p[block, i * 16 + k], 1), :]
                return inner

            lax.fori_loop(0, rows // 16, row, 0)
            plain[block] = picked[...].astype(jnp.bfloat16)
            return carry

        lax.fori_loop(0, COLS, slab, 0)
        few = index_w.shape[1]

        def slab_w(block, carry):
            def row(i, inner):
                for k in range(16):
                    picked[pl.ds(i * 16 + k, 1), :] = cells[pl.ds(index_w[block, i * 16 + k], 1), :]
                return inner

            lax.fori_loop(0, few // 16, row, 0)
            weighted[block] = (picked[:few] * weight).astype(jnp.bfloat16)
            return carry

        lax.fori_loop(0, ROWS, slab_w, 0)


def spectra(val_wave, cond_wave, val_energy, cond_energy, band_owner):
    index_p, _ = orbit_lists(G_COL, COLS)
    index_w, _ = orbit_lists(G_ROW, ROWS)
    tables = dft_tables()
    smem = pl.BlockSpec(memory_space=pltpu.SMEM)
    whole = pl.BlockSpec((16 * MAGS, 4 * GRID), lambda i: (0, 0))
    return pl.pallas_call(
        spectrum_kernel,
        grid=(4,),
        in_specs=[smem] * 5
        + [
            pl.BlockSpec((2, GRID, GRID, LANES), lambda i: (i, 0, 0, 0)),
            pl.BlockSpec((1, GRID, GRID, LANES), lambda i: (0, 0, 0, 0)),
            whole, whole, whole,
        ],
        out_specs=[
            pl.BlockSpec((COLS, index_p.shape[1], LANES), lambda i: (0, 0, 0)),
            pl.BlockSpec((ROWS, index_w.shape[1], LANES), lambda i: (0, 0, 0)),
        ],
        out_shape=[
            jax.ShapeDtypeStruct((COLS, index_p.shape[1], LANES), jnp.bfloat16),
            jax.ShapeDtypeStruct((ROWS, index_w.shape[1], LANES), jnp.bfloat16),
        ],
        scratch_shapes=[
            pltpu.VMEM((10, 4 * GRID, 2 * LANES), jnp.bfloat16),
            pltpu.VMEM((10, 4 * GRID, 2 * LANES), jnp.bfloat16),
            pltpu.VMEM((4, CELLS, 2 * LANES), jnp.bfloat16),
            pltpu.VMEM((4, CELLS, 2 * LANES), jnp.bfloat16),
            pltpu.VMEM((MAGS, LANES, 512), jnp.float32),
            pltpu.VMEM((MAGS * CELLS, LANES), jnp.float32),
            pltpu.VMEM((index_p.shape[1], LANES), jnp.float32),
        ],
        compiler_params=pltpu.CompilerParams(vmem_limit_bytes=48 * 2**20),
        name="spectra",
    )(
        band_owner, cond_energy, val_energy, jnp.asarray(index_p), jnp.asarray(index_w),
        val_wave, cond_wave, *(jnp.asarray(table) for table in tables),
    )


def place_kernel(points, codes, slabs, fold, out):
    point = points[...]
    a, b, c = point >> 12, (point >> 6) & 63, point & 63
    half = GRID // 2
    code = (jnp.where(a > half, GRID - a, a) * GRID + jnp.where(b > half, GRID - b, b)) * GRID
    code = code + jnp.where(c > half, GRID - c, c)
    octant = (
        jnp.where(a > half, 4, 0) + jnp.where(b > half, 2, 0) + jnp.where(c > half, 1, 0)
    )
    hot = (code == codes[...]).astype(jnp.bfloat16)
    lane = lax.broadcasted_iota(jnp.int32, (1, LANES), 1)
    own = octant == (lane >> 5) * 2 + lane % 2
    total = None
    for source in range(slabs.shape[0]):
        row = dot_nn(hot, slabs[source])
        row = jnp.where(own, row, 0.0).astype(jnp.bfloat16)
        term = dot_nn(row, fold[source])
        total = term if total is None else total + term
    out[...] = total.astype(jnp.bfloat16)


def place(points, codes, slabs, tile):
    count, rows, _ = slabs.shape
    width = points.shape[0]
    fold = np.zeros((count, LANES, count * 16), ml_dtypes.bfloat16)
    lane = np.arange(LANES)
    for source in range(count):
        fold[source, lane, source * 16 + (lane >> 3) % 4 * 4 + (lane >> 1) % 4] = 1.0
    return pl.pallas_call(
        place_kernel,
        grid=(width // tile,),
        in_specs=[
            pl.BlockSpec((tile, 1), lambda i: (i, 0)),
            pl.BlockSpec((1, rows), lambda i: (0, 0)),
            pl.BlockSpec((count, rows, LANES), lambda i: (0, 0, 0)),
            pl.BlockSpec((count, LANES, count * 16), lambda i: (0, 0, 0)),
        ],
        out_specs=pl.BlockSpec((tile, count * 16), lambda i: (i, 0)),
        out_shape=jax.ShapeDtypeStruct((width, count * 16), jnp.bfloat16),
        compiler_params=pltpu.CompilerParams(vmem_limit_bytes=48 * 2**20),
        name="place",
    )(points.reshape(width, 1), codes, slabs, jnp.asarray(fold))


def product_kernel(left, panels, out):
    total = None
    depth = panels.shape[2]
    for source in range(panels.shape[0]):
        term = dot_nt(left[:, source * depth : (source + 1) * depth], panels[source])
        total = term if total is None else total + term
    out[...] = total.reshape(out.shape)


def product(left, panels, tile):
    count, width, depth = panels.shape
    return pl.pallas_call(
        product_kernel,
        grid=(width // tile,),
        in_specs=[
            pl.BlockSpec((2 * G_ROW, count * depth), lambda i: (0, 0)),
            pl.BlockSpec((count, tile, depth), lambda i: (0, i, 0)),
        ],
        out_specs=pl.BlockSpec((2, G_ROW, tile), lambda i: (0, 0, i)),
        out_shape=jax.ShapeDtypeStruct((2, G_ROW, width), jnp.float32),
        compiler_params=pltpu.CompilerParams(vmem_limit_bytes=48 * 2**20),
        name="product",
    )(left, panels)


def on_device(val_wave, cond_wave, val_energy, cond_energy, band_owner, grid_map):
    row = lax.axis_index("row")
    col = lax.axis_index("col")
    plain, weighted = spectra(val_wave, cond_wave, val_energy, cond_energy, band_owner)
    _, codes_p = orbit_lists(G_COL, COLS)
    _, codes_w = orbit_lists(G_ROW, ROWS)
    weighted = lax.all_to_all(weighted, "row", split_axis=0, concat_axis=0, tiled=True)
    plain = lax.all_to_all(plain, "col", split_axis=0, concat_axis=0, tiled=True)
    points_w = lax.dynamic_slice(grid_map, (row * G_ROW,), (G_ROW,))
    points_p = lax.dynamic_slice(grid_map, (col * G_COL,), (G_COL,))
    left = place(points_w, jnp.asarray(codes_w)[row], weighted, G_ROW)
    panel = place(points_p, jnp.asarray(codes_p)[col], plain, 384)
    left = lax.all_gather(left, "col", axis=0)
    panels = lax.all_gather(panel, "row", axis=0)
    left = left.reshape(COLS, G_ROW, ROWS, 8, 2).transpose(1, 2, 0, 3, 4)
    left_im = jnp.stack([left[..., 1], -left[..., 0]], -1)
    left = jnp.stack([left, left_im]).reshape(2 * G_ROW, ROWS * COLS * 16)
    return product(left, panels, 384)


def solution(mesh):
    in_specs = (P(), P(("row", "col"), None, None, None), P(), P(), P(("row", "col")), P())
    out_specs = P(None, "row", "col")
    return jax.shard_map(
        on_device, mesh=mesh, in_specs=in_specs, out_specs=out_specs, check_vma=False
    )
```

```python
import functools
import math

import jax
import jax.numpy as jnp
import ml_dtypes
import numpy as np
from jax import lax
from jax.experimental import pallas as pl
from jax.experimental.pallas import tpu as pltpu
from jax.sharding import PartitionSpec as P

GRID = 64
NG = 30720
SLAB = 2048
ROWS = 8
COLS = 16
G_COL = NG // COLS
G_ROW = SLAB // ROWS
MAGS = 20
CELLS = MAGS * MAGS
LANES = 128


def shells():
    points = np.arange(GRID)
    freq = np.where(points < GRID // 2, points, points - GRID)
    square = freq * freq
    length = (square[:, None, None] + square[None, :, None] + square[None, None, :]).ravel()
    length = np.sort(length, kind="stable")
    assert length[NG - 1] < MAGS * MAGS
    return length


def orbit_lists(width, count):
    length = shells()
    mags = np.arange(MAGS)
    a, b, c = np.meshgrid(mags, mags, mags, indexing="ij")
    a, b, c = a.ravel(), b.ravel(), c.ravel()
    square = a * a + b * b + c * c
    source = c * CELLS + (b // 4) * (4 * MAGS) + a * 4 + b % 4
    code = (a * GRID + b) * GRID + c
    order = np.argsort(square, kind="stable")
    lists = []
    for block in range(count):
        least, most = length[block * width], length[(block + 1) * width - 1]
        lists.append(order[(square[order] >= least) & (square[order] <= most)])
    rows = -(-max(len(picked) for picked in lists) // 16) * 16
    index = np.zeros((count, rows), np.int32)
    codes = np.full((count, 1, rows), -1, np.int32)
    for block, picked in enumerate(lists):
        index[block, : len(picked)] = source[picked]
        codes[block, 0, : len(picked)] = code[picked]
    return index, codes, [square[picked] for picked in lists]


def windows(width, count, tile):
    length = shells()
    _, codes, squares = orbit_lists(width, count)
    starts, ends = [], []
    for at in range(0, width, tile):
        first, last = [], []
        for block, square in enumerate(squares):
            first.append(np.searchsorted(square, length[block * width + at], "left"))
            last.append(np.searchsorted(square, length[block * width + at + tile - 1], "right"))
        starts.append(int(min(first)) // 16 * 16)
        ends.append(int(max(last)))
    rows = max(-(-(end - start) // 16) * 16 for start, end in zip(starts, ends))
    return [min(start, codes.shape[2] - rows) for start in starts], rows


def split_table(table):
    high = table.astype(ml_dtypes.bfloat16)
    low = (table - high.astype(np.float64)).astype(ml_dtypes.bfloat16)
    return np.concatenate([high, low], 0)


def dft_tables():
    point = np.arange(GRID)
    mag = np.arange(MAGS)
    angle = (mag[:, None] * point[None, :] % GRID) * (2.0 * math.pi / GRID)
    parts = np.stack([np.cos(angle), np.sin(angle)])
    table_b = np.zeros((2, MAGS // 4, 4, 4, 4, GRID))
    for a in range(4):
        table_b[:, :, a, :, a, :] = parts.reshape(2, MAGS // 4, 4, GRID)
    table_a = np.zeros((2, MAGS, 4, GRID, 4))
    for b in range(4):
        table_a[:, :, b, :, b] = parts
    table_c = np.zeros((MAGS, 2, 2, 2, 2, 2, GRID))
    for v in range(2):
        for sign in range(2):
            turn = 1.0 - 2.0 * sign
            table_c[:, v, 0, sign, 0, v] = parts[0]
            table_c[:, v, 0, sign, 1, v] = turn * parts[1]
            table_c[:, v, 1, sign, 1, v] = parts[0]
            table_c[:, v, 1, sign, 0, v] = -turn * parts[1]
    table_c = table_c * (1.0 / float(GRID) ** 1.5)
    return (
        split_table(table_b.reshape(8 * MAGS, 4 * GRID)),
        split_table(table_a.reshape(8 * MAGS, 4 * GRID)),
        split_table(table_c.reshape(8 * MAGS, 4 * GRID)),
    )


def dot_nn(left, right):
    return lax.dot_general(
        left, right, (((1,), (0,)), ((), ())), preferred_element_type=jnp.float32
    )


def dot_nt(left, right):
    return lax.dot_general(
        left, right, (((1,), (1,)), ((), ())), preferred_element_type=jnp.float32
    )


def halves(value):
    high = value.astype(jnp.bfloat16)
    return high, (value - high.astype(jnp.float32)).astype(jnp.bfloat16)


def three(dot, table, high, low):
    rows = table.shape[0] // 2
    both = dot(table, high)
    return both[:rows] + both[rows:] + dot(table[:rows], low)


def signs(both, rows):
    cos_re, cos_im = both[:rows, :LANES], both[:rows, LANES:]
    sin_re, sin_im = both[rows:, :LANES], both[rows:, LANES:]
    plus = jnp.concatenate([cos_re + sin_im, cos_im - sin_re], 1)
    minus = jnp.concatenate([cos_re - sin_im, cos_im + sin_re], 1)
    return plus, minus


def spectrum_kernel(
    owner, cond_energy, val_energy, index_p, index_w,
    val, cond, table_b, table_a, table_c,
    plain, weighted,
    slots, zh, zl, uh, ul, sums, cells, picked,
):
    step = pl.program_id(0)
    block = 4 * GRID
    first = lax.broadcasted_iota(jnp.int32, (block, LANES), 1) < GRID
    tb = table_b[...]

    @pl.when(step == 0)
    def _():
        def widen(t, carry):
            slot = cond[0, pl.ds(t * 4, 4)].reshape(block, LANES).astype(jnp.float32)
            slot_t = pltpu.roll(slot, GRID, 1)
            slots[t, 0] = jnp.where(first, slot, slot_t)
            slots[t, 1] = jnp.where(first, slot_t, slot)
            return carry

        lax.fori_loop(0, GRID // 4, widen, 0)

    def along_b(t, carry):
        rows = pl.ds(t * 4, 4)
        one = val[0, rows].reshape(block, LANES).astype(jnp.float32)
        two = val[1, rows].reshape(block, LANES).astype(jnp.float32)
        one_t = pltpu.roll(one, GRID, 1)
        two_t = pltpu.roll(two, GRID, 1)
        slot_re, slot_im = slots[t, 0], slots[t, 1]
        val_re = jnp.where(first, one, two_t)
        val_im = jnp.where(first, one_t, two)
        dens_re = val_re * slot_re + val_im * slot_im
        dens_im = val_re * slot_im - val_im * slot_re
        high, low = halves(jnp.concatenate([dens_re, dens_im], 1))
        both = three(dot_nn, tb, high, low)
        out = pl.ds(pl.multiple_of(t * 16, 16), 16)
        for sign, value in enumerate(signs(both, 4 * MAGS)):
            high, low = halves(value)
            for group in range(MAGS // 4):
                zh[sign * 5 + group, out, :] = high[group * 16 : group * 16 + 16]
                zl[sign * 5 + group, out, :] = low[group * 16 : group * 16 + 16]
        return carry

    lax.fori_loop(0, GRID // 4, along_b, 0, unroll=2)
    ta = table_a[...]

    def along_a(group, carry):
        out = pl.ds(pl.multiple_of(group * 80, 16), 80)
        for sign_b in range(2):
            both = three(dot_nn, ta, zh[sign_b * 5 + group], zl[sign_b * 5 + group])
            for sign_a, value in enumerate(signs(both, 4 * MAGS)):
                high, low = halves(value)
                uh[sign_a * 2 + sign_b, out, :] = high
                ul[sign_a * 2 + sign_b, out, :] = low
        return carry

    lax.fori_loop(0, MAGS // 4, along_a, 0, unroll=True)
    tc = table_c[...]

    def along_c(pair, carry):
        value = three(dot_nt, tc, uh[pair], ul[pair])
        value = value.reshape(MAGS, 8, CELLS)
        sums[:, pl.ds(pl.multiple_of((pair * 4 + step) * 8, 8), 8), :CELLS] = value
        return carry

    lax.fori_loop(0, 4, along_c, 0, unroll=2)

    @pl.when(step == pl.num_programs(0) - 1)
    def _():
        def turn(mag, carry):
            value = jnp.transpose(sums[mag], (1, 0))
            cells[pl.ds(pl.multiple_of(mag * CELLS, 8), CELLS), :] = value[:CELLS]
            return carry

        lax.fori_loop(0, MAGS, turn, 0, unroll=2)
        lane = lax.broadcasted_iota(jnp.int32, (1, LANES), 1)
        band = (lane >> 3) % 4 * 2 + (lane >> 2) % 2
        gap = jnp.zeros((1, LANES), jnp.float32)
        energy = cond_energy[owner[0]]
        for v in range(8):
            gap = jnp.where(band == v, energy - val_energy[v], gap)
        weight = -2.0 / (math.sqrt(8 * LANES) * gap)
        def gather(index, count):
            def row(i, carry):
                for k in range(64):
                    picked[pl.ds(i * 64 + k, 1), :] = cells[pl.ds(index[i * 64 + k], 1), :]
                return carry

            lax.fori_loop(0, count // 64, row, 0)

        gather(index_p, plain.shape[0] * plain.shape[1])
        plain[...] = picked[...].astype(jnp.bfloat16).reshape(plain.shape)
        count = weighted.shape[0] * weighted.shape[1]
        gather(index_w, count)
        weighted[...] = (picked[:count] * weight).astype(jnp.bfloat16).reshape(weighted.shape)


def spectra(val_wave, cond_wave, val_energy, cond_energy, band_owner):
    index_p, _, _ = orbit_lists(G_COL, COLS)
    index_w, _, _ = orbit_lists(G_ROW, ROWS)
    tables = dft_tables()
    smem = pl.BlockSpec(memory_space=pltpu.SMEM)
    whole = pl.BlockSpec((16 * MAGS, 4 * GRID), lambda i: (0, 0))
    return pl.pallas_call(
        spectrum_kernel,
        grid=(4,),
        in_specs=[smem] * 5
        + [
            pl.BlockSpec((2, GRID, GRID, LANES), lambda i: (i, 0, 0, 0)),
            pl.BlockSpec((1, GRID, GRID, LANES), lambda i: (0, 0, 0, 0)),
            whole, whole, whole,
        ],
        out_specs=[
            pl.BlockSpec((COLS, index_p.shape[1], LANES), lambda i: (0, 0, 0)),
            pl.BlockSpec((ROWS, index_w.shape[1], LANES), lambda i: (0, 0, 0)),
        ],
        out_shape=[
            jax.ShapeDtypeStruct((COLS, index_p.shape[1], LANES), jnp.bfloat16),
            jax.ShapeDtypeStruct((ROWS, index_w.shape[1], LANES), jnp.bfloat16),
        ],
        scratch_shapes=[
            pltpu.VMEM((GRID // 4, 2, 4 * GRID, LANES), jnp.float32),
            pltpu.VMEM((10, 4 * GRID, 2 * LANES), jnp.bfloat16),
            pltpu.VMEM((10, 4 * GRID, 2 * LANES), jnp.bfloat16),
            pltpu.VMEM((4, CELLS, 2 * LANES), jnp.bfloat16),
            pltpu.VMEM((4, CELLS, 2 * LANES), jnp.bfloat16),
            pltpu.VMEM((MAGS, LANES, 512), jnp.float32),
            pltpu.VMEM((MAGS * CELLS, LANES), jnp.float32),
            pltpu.VMEM((index_p.size, LANES), jnp.float32),
        ],
        compiler_params=pltpu.CompilerParams(vmem_limit_bytes=48 * 2**20),
        name="spectra",
    )(
        band_owner, cond_energy, val_energy, jnp.asarray(index_p.ravel()), jnp.asarray(index_w.ravel()),
        val_wave, cond_wave, *(jnp.asarray(table) for table in tables),
    )


def placed(point, codes, slabs, fold):
    a, b, c = point >> 12, (point >> 6) & 63, point & 63
    half = GRID // 2
    code = (jnp.where(a > half, GRID - a, a) * GRID + jnp.where(b > half, GRID - b, b)) * GRID
    code = code + jnp.where(c > half, GRID - c, c)
    octant = (
        jnp.where(a > half, 4, 0) + jnp.where(b > half, 2, 0) + jnp.where(c > half, 1, 0)
    )
    hot = (code == codes).astype(jnp.bfloat16)
    lane = lax.broadcasted_iota(jnp.int32, (1, 2 * LANES), 1) % LANES
    own = octant == (lane >> 5) * 2 + lane % 2
    rows = []
    for pair in range(len(slabs) // 2):
        both = jnp.concatenate([slabs[2 * pair], slabs[2 * pair + 1]], 1)
        rows.append(jnp.where(own, dot_nn(hot, both), 0.0).astype(jnp.bfloat16))
    return dot_nn(jnp.concatenate(rows, 1), fold)


def fold_table(count):
    fold = np.zeros((count, LANES, count * 16), ml_dtypes.bfloat16)
    lane = np.arange(LANES)
    for source in range(count):
        fold[source, lane, source * 16 + (lane >> 3) % 4 * 4 + (lane >> 1) % 4] = 1.0
    return fold.reshape(count * LANES, count * 16)


def turn_table():
    table = np.zeros((2 * LANES, 2 * LANES), ml_dtypes.bfloat16)
    lane = np.arange(0, 2 * LANES, 2)
    table[lane + 1, lane] = 1.0
    table[lane, lane + 1] = -1.0
    return table


TILE = 384
TILES = G_COL // TILE
KINDS = 9


def exchange_kernel(
    points_p, points_w, codes_p, codes_w, plain, weighted, fold_p, fold_w, turn,
    out,
    slabs, slabs_w, lefts, left, panels, stage,
    col_send, col_recv, row_send, row_recv, left_send, left_recv, move_send, move_recv, own_sem, out_sem,
):
    row, col = lax.axis_index("row"), lax.axis_index("col")
    z, y_hi = row // 2, lax.rem(row, 2)
    x, y_lo, core = col // 4, lax.rem(col // 2, 2), lax.rem(col, 2)
    up, down, far = lax.rem(z + 1, 4), lax.rem(z + 3, 4), lax.rem(z + 2, 4)
    above, below = (up * 2 + y_hi, col), (down * 2 + y_hi, col)
    across_row = z * 2 + 1 - y_hi
    across = (across_row, col)
    slot = core * 8 + col // 2

    def push(src, dst, send, recv, device):
        return pltpu.make_async_remote_copy(
            src_ref=src, dst_ref=dst, send_sem=send, recv_sem=recv,
            device_id=device, device_id_type=pl.DeviceIdType.MESH,
        )

    barrier = pltpu.get_barrier_semaphore()
    for i in range(1, COLS):
        pl.semaphore_signal(
            barrier, inc=1, device_id=(row, lax.rem(col + i, COLS)),
            device_id_type=pl.DeviceIdType.MESH,
        )
    for i in range(1, ROWS):
        pl.semaphore_signal(
            barrier, inc=1, device_id=(lax.rem(row + i, ROWS), col),
            device_id_type=pl.DeviceIdType.MESH,
        )
    pl.semaphore_wait(barrier, COLS + ROWS - 2)

    started = []
    row_copies, col_copies = [], []
    for i in range(1, ROWS):
        to = lax.rem(row + i, ROWS)
        copy = push(weighted.at[to], slabs_w.at[row], row_send.at[i], row_recv.at[i], (to, col))
        copy.start()
        row_copies.append(copy)
    for i in range(1, COLS):
        to = lax.rem(col + i, COLS)
        copy = push(plain.at[to], slabs.at[slot], col_send.at[i], col_recv.at[i], (row, to))
        copy.start()
        col_copies.append(copy)
    own_p = pltpu.make_async_copy(plain.at[col], slabs.at[slot], own_sem.at[0])
    own_w = pltpu.make_async_copy(weighted.at[row], slabs_w.at[row], own_sem.at[1])
    own_p.start()
    own_w.start()
    own_w.wait()
    for copy in row_copies:
        copy.wait_recv()
    block = placed(points_w[...], codes_w[...], [slabs_w[i] for i in range(ROWS)], fold_w[...])
    lefts[slot] = jnp.transpose(block, (1, 0)).astype(jnp.bfloat16)
    beside = push(
        lefts.at[slot], lefts.at[slot], left_send.at[0], left_recv.at[0],
        (row, (x * 2 + 1 - y_lo) * 2 + core),
    )
    beside.start()

    own_p.wait()
    for copy in col_copies:
        copy.wait_recv()

    def part(source, tile, half=None):
        if half is None:
            rows = pl.ds(tile * TILE, TILE)
        else:
            rows = pl.ds(tile * TILE + half * (TILE // 2), TILE // 2)
        return panels.at[source].at[rows]

    moves = {}

    def move(tile, kind, source, device, half=None):
        copy = push(
            part(source, tile, half), part(source, tile, half),
            move_send.at[tile * KINDS + kind], move_recv.at[tile * KINDS + kind], device,
        )
        copy.start()
        moves[tile, kind] = copy

    starts, span = windows(G_COL, COLS, TILE)
    for tile in range(TILES):
        window = slice(starts[tile], starts[tile] + span)
        block = placed(
            points_p[tile * TILE : (tile + 1) * TILE], codes_p[:, window],
            [slabs[i, window] for i in range(COLS)], fold_p[...],
        )
        panels[row, tile * TILE : (tile + 1) * TILE, :] = block.astype(jnp.bfloat16)
        move(tile, 0, row, across)
        move(tile, 1, row, above)
        move(tile, 2, row, below)

    first, second = range(3), range(3, TILES)

    def pass_on(tile, y, kinds):
        moves[tile, kinds[0]].wait_recv()
        move(tile, kinds[2], down * 2 + y, (up * 2 + y_hi, col), 0)
        moves[tile, kinds[1]].wait_recv()
        move(tile, kinds[3], up * 2 + y, (down * 2 + y_hi, col), 1)

    for tile in first:
        moves[tile, 0].wait_recv()
        move(tile, 5, across_row, above)
        move(tile, 6, across_row, below)
        pass_on(tile, y_hi, (1, 2, 3, 4))
    beside.wait_recv()
    spread = []
    for i in range(1, 4):
        to = lax.rem(x + i, 4)
        pair = lefts.at[pl.ds(core * 8 + x * 2, 2)]
        copy = push(pair, pair, left_send.at[i], left_recv.at[i], (row, (to * 2 + y_lo) * 2 + core))
        copy.start()
        spread.append(copy)
    for tile in second:
        pass_on(tile, y_hi, (1, 2, 3, 4))
        move(tile, 5, down * 2 + y_hi, across)
        move(tile, 6, up * 2 + y_hi, across)
    for tile in first:
        pass_on(tile, 1 - y_hi, (5, 6, 7, 8))
    for copy in spread:
        copy.wait_recv()
    octet = lefts.at[pl.ds(core * 8, 8)]
    twin = push(octet, octet, left_send.at[4], left_recv.at[4], (row, col + 1 - 2 * core))
    twin.start()
    for tile in second:
        moves[tile, 3].wait_recv()
        move(tile, 7, far * 2 + y_hi, across, 0)
        moves[tile, 4].wait_recv()
        move(tile, 8, far * 2 + y_hi, across, 1)
    twin.wait_recv()
    for source in range(ROWS):
        block = lefts[:, source * 16 : source * 16 + 16, :].reshape(2 * LANES, G_ROW)
        block = jnp.transpose(block.astype(jnp.float32), (1, 0)).astype(jnp.bfloat16)
        lanes = slice(source * 2 * LANES, (source + 1) * 2 * LANES)
        left[:G_ROW, lanes] = block
        left[G_ROW:, lanes] = dot_nn(block, turn[...]).astype(jnp.bfloat16)

    outs = []
    for tile in range(TILES):
        for kind in (3, 4, 7, 8) if tile in first else (0, 5, 6, 7, 8):
            moves[tile, kind].wait_recv()
        total = None
        for source in range(ROWS):
            term = dot_nt(
                left[:, source * 2 * LANES : (source + 1) * 2 * LANES],
                panels[source, tile * TILE : (tile + 1) * TILE, :],
            )
            total = term if total is None else total + term
        if tile >= 2:
            outs[tile - 2].wait()
        stage[tile % 2] = total.reshape(2, G_ROW, TILE)
        copy = pltpu.make_async_copy(
            stage.at[tile % 2], out.at[:, :, pl.ds(tile * TILE, TILE)], out_sem.at[tile % 2]
        )
        copy.start()
        outs.append(copy)
    for copy in row_copies + col_copies + [beside] + spread + [twin]:
        copy.wait_send()
    for copy in moves.values():
        copy.wait_send()
    outs[-2].wait()
    outs[-1].wait()


def exchange(points_p, points_w, codes_p, codes_w, plain, weighted):
    vmem = pl.BlockSpec(memory_space=pltpu.VMEM)
    dma = pltpu.SemaphoreType.DMA
    return pl.pallas_call(
        exchange_kernel,
        in_specs=[vmem] * 9,
        out_specs=pl.BlockSpec(memory_space=pl.ANY),
        out_shape=jax.ShapeDtypeStruct((2, G_ROW, G_COL), jnp.float32),
        scratch_shapes=[
            pltpu.VMEM(plain.shape, jnp.bfloat16),
            pltpu.VMEM(weighted.shape, jnp.bfloat16),
            pltpu.VMEM((COLS, LANES, G_ROW), jnp.bfloat16),
            pltpu.VMEM((2 * G_ROW, ROWS * 2 * LANES), jnp.bfloat16),
            pltpu.VMEM((ROWS, G_COL, 2 * LANES), jnp.bfloat16),
            pltpu.VMEM((2, 2, G_ROW, TILE), jnp.float32),
            dma((COLS,)), dma((COLS,)), dma((ROWS,)), dma((ROWS,)), dma((5,)), dma((5,)),
            dma((TILES * KINDS,)), dma((TILES * KINDS,)), dma((2,)), dma((2,)),
        ],
        compiler_params=pltpu.CompilerParams(
            collective_id=0, has_side_effects=True, vmem_limit_bytes=56 * 2**20
        ),
        name="exchange",
    )(
        points_p, points_w, codes_p, codes_w, plain, weighted,
        jnp.asarray(fold_table(COLS)), jnp.asarray(fold_table(ROWS)), jnp.asarray(turn_table()),
    )


def on_device(val_wave, cond_wave, val_energy, cond_energy, band_owner, grid_map):
    row = lax.axis_index("row")
    col = lax.axis_index("col")
    plain, weighted = spectra(val_wave, cond_wave, val_energy, cond_energy, band_owner)
    codes_p = orbit_lists(G_COL, COLS)[1]
    codes_w = orbit_lists(G_ROW, ROWS)[1]
    points_p = lax.dynamic_slice(grid_map, (col * G_COL,), (G_COL,)).reshape(G_COL, 1)
    points_w = lax.dynamic_slice(grid_map, (row * G_ROW,), (G_ROW,)).reshape(G_ROW, 1)
    return exchange(
        points_p, points_w, jnp.asarray(codes_p)[col], jnp.asarray(codes_w)[row], plain, weighted
    )


def solution(mesh):
    in_specs = (P(), P(("row", "col"), None, None, None), P(), P(), P(("row", "col")), P())
    out_specs = P(None, "row", "col")
    return jax.shard_map(
        on_device, mesh=mesh, in_specs=in_specs, out_specs=out_specs, check_vma=False
    )
```

```python
import math

import jax
import jax.numpy as jnp
import ml_dtypes
import numpy as np
from jax import lax
from jax.experimental import pallas as pl
from jax.experimental.pallas import tpu as pltpu
from jax.sharding import PartitionSpec as P

GRID = 64
NG = 30720
SLAB = 2048
ROWS = 8
COLS = 16
G_COL = NG // COLS
G_ROW = SLAB // ROWS
MAGS = 20
CELLS = MAGS * MAGS
LANES = 128


def shells():
    points = np.arange(GRID)
    freq = np.where(points < GRID // 2, points, points - GRID)
    square = freq * freq
    length = (square[:, None, None] + square[None, :, None] + square[None, None, :]).ravel()
    length = np.sort(length, kind="stable")
    assert length[NG - 1] < MAGS * MAGS
    return length


def orbit_lists(width, count):
    length = shells()
    mags = np.arange(MAGS)
    a, b, c = np.meshgrid(mags, mags, mags, indexing="ij")
    a, b, c = a.ravel(), b.ravel(), c.ravel()
    square = a * a + b * b + c * c
    source = c * CELLS + (b // 4) * (4 * MAGS) + a * 4 + b % 4
    code = (a * GRID + b) * GRID + c
    order = np.argsort(square, kind="stable")
    lists = []
    for block in range(count):
        least, most = length[block * width], length[(block + 1) * width - 1]
        lists.append(order[(square[order] >= least) & (square[order] <= most)])
    rows = -(-max(len(picked) for picked in lists) // 16) * 16
    index = np.zeros((count, rows), np.int32)
    codes = np.full((count, 1, rows), -1, np.int32)
    for block, picked in enumerate(lists):
        index[block, : len(picked)] = source[picked]
        codes[block, 0, : len(picked)] = code[picked]
    return index, codes, [square[picked] for picked in lists]


def split_table(table):
    high = table.astype(ml_dtypes.bfloat16)
    low = (table - high.astype(np.float64)).astype(ml_dtypes.bfloat16)
    return np.concatenate([high, low], 0)


def dft_tables():
    point = np.arange(GRID)
    mag = np.arange(MAGS)
    angle = (mag[:, None] * point[None, :] % GRID) * (2.0 * math.pi / GRID)
    parts = np.stack([np.cos(angle), np.sin(angle)])
    table_b = np.zeros((2, MAGS // 4, 4, 4, 4, GRID))
    for a in range(4):
        table_b[:, :, a, :, a, :] = parts.reshape(2, MAGS // 4, 4, GRID)
    table_a = np.zeros((2, MAGS, 4, GRID, 4))
    for b in range(4):
        table_a[:, :, b, :, b] = parts
    table_c = np.zeros((MAGS, 2, 2, 2, 2, 2, GRID))
    for v in range(2):
        for sign in range(2):
            turn = 1.0 - 2.0 * sign
            table_c[:, v, 0, sign, 0, v] = parts[0]
            table_c[:, v, 0, sign, 1, v] = turn * parts[1]
            table_c[:, v, 1, sign, 1, v] = parts[0]
            table_c[:, v, 1, sign, 0, v] = -turn * parts[1]
    table_c = table_c * (1.0 / float(GRID) ** 1.5)
    return (
        split_table(table_b.reshape(8 * MAGS, 4 * GRID)),
        split_table(table_a.reshape(8 * MAGS, 4 * GRID)),
        split_table(table_c.reshape(8 * MAGS, 4 * GRID)),
    )


def dot_nn(left, right):
    return lax.dot_general(
        left, right, (((1,), (0,)), ((), ())), preferred_element_type=jnp.float32
    )


def dot_nt(left, right):
    return lax.dot_general(
        left, right, (((1,), (1,)), ((), ())), preferred_element_type=jnp.float32
    )


def halves(value):
    high = value.astype(jnp.bfloat16)
    return high, (value - high.astype(jnp.float32)).astype(jnp.bfloat16)


def three(dot, table, high, low):
    rows = table.shape[0] // 2
    both = dot(table, high)
    return both[:rows] + both[rows:] + dot(table[:rows], low)


def signs(both, rows):
    cos_re, cos_im = both[:rows, :LANES], both[:rows, LANES:]
    sin_re, sin_im = both[rows:, :LANES], both[rows:, LANES:]
    plus = jnp.concatenate([cos_re + sin_im, cos_im - sin_re], 1)
    minus = jnp.concatenate([cos_re - sin_im, cos_im + sin_re], 1)
    return plus, minus


def windows(width, count, tile):
    length = shells()
    _, codes, squares = orbit_lists(width, count)
    starts, ends = [], []
    for at in range(0, width, tile):
        first, last = [], []
        for block, square in enumerate(squares):
            first.append(np.searchsorted(square, length[block * width + at], "left"))
            last.append(np.searchsorted(square, length[block * width + at + tile - 1], "right"))
        starts.append(int(min(first)) // 32 * 16)
        ends.append(-(-int(max(last)) // 2))
    rows = max(-(-(end - start) // 16) * 16 for start, end in zip(starts, ends))
    return [min(start, codes.shape[2] // 2 - rows) for start in starts], rows


def paired(codes):
    return np.stack([codes[:, 0, 0::2], codes[:, 0, 1::2]], 1)


def fold_table(count, width):
    fold = np.zeros((count, LANES, width), ml_dtypes.bfloat16)
    lane = np.arange(LANES)
    for source in range(count):
        fold[source, lane, source * 8 + (lane >> 1) % 8] = 1.0
    return fold.reshape(count * LANES, width)


def turn_table():
    table = np.zeros((LANES, LANES), ml_dtypes.bfloat16)
    lane = np.arange(0, LANES, 2)
    table[lane + 1, lane] = 1.0
    table[lane, lane + 1] = -1.0
    return table


def placed(point, codes, slabs, fold):
    a, b, c = point >> 12, (point >> 6) & 63, point & 63
    half = GRID // 2
    code = (jnp.where(a > half, GRID - a, a) * GRID + jnp.where(b > half, GRID - b, b)) * GRID
    code = code + jnp.where(c > half, GRID - c, c)
    odd = jnp.where(code == codes[1:2], 1.0, 0.0)
    hot = jnp.where(code == codes[0:1], 1.0, odd).astype(jnp.bfloat16)
    key = (
        jnp.where(jnp.sum(odd, axis=1, keepdims=True) > 0.5, 8, 0)
        + jnp.where(a > half, 4, 0) + jnp.where(b > half, 2, 0) + jnp.where(c > half, 1, 0)
    )
    lane = lax.broadcasted_iota(jnp.int32, (1, 2 * LANES), 1) % LANES
    own = key == (lane >> 4) * 2 + lane % 2
    rows = []
    for pair in range(len(slabs) // 2):
        both = jnp.concatenate([slabs[2 * pair], slabs[2 * pair + 1]], 1)
        rows.append(jnp.where(own, dot_nn(hot, both), 0.0).astype(jnp.bfloat16))
    return dot_nn(jnp.concatenate(rows, 1), fold)


TILE = 384
TILES = G_COL // TILE
KINDS = 9


def whole_kernel(
    owner, cond_energy, val_energy, index_p, index_w,
    grid_map, codes_p, codes_w, table_b, table_a, table_c, fold_p, fold_w, turn, val_hbm, cond_hbm,
    out,
    val, cond, slots, zh, zl, uh, ul, sums, cells, picked, points_p, points_w, lines,
    plain, weighted, slabs, slabs_w, lefts, lefts_wide, left, panels, totals,
    val_sem, cond_sem, own_sem, out_sem,
    col_send, col_recv, row_send, row_recv, left_send, left_recv, move_send, move_recv,
):
    row, col = lax.axis_index("row"), lax.axis_index("col")
    z, y_hi = row // 2, lax.rem(row, 2)
    x, y_lo, core = col // 4, lax.rem(col // 2, 2), lax.rem(col, 2)
    up, down, far = lax.rem(z + 1, 4), lax.rem(z + 3, 4), lax.rem(z + 2, 4)
    above, below = (up * 2 + y_hi, col), (down * 2 + y_hi, col)
    across_row = z * 2 + 1 - y_hi
    across = (across_row, col)
    slot = core * 8 + col // 2
    mesh = pl.DeviceIdType.MESH

    fetch_cond = pltpu.make_async_copy(cond_hbm, cond, cond_sem)
    fetch_cond.start()
    fetch_val = []
    for pair in range(4):
        copy = pltpu.make_async_copy(val_hbm.at[pl.ds(2 * pair, 2)], val.at[pair], val_sem.at[pair])
        copy.start()
        fetch_val.append(copy)

    barrier = pltpu.get_barrier_semaphore()
    for i in range(1, COLS):
        pl.semaphore_signal(barrier, inc=1, device_id=(row, lax.rem(col + i, COLS)), device_id_type=mesh)
    for i in range(1, ROWS):
        pl.semaphore_signal(barrier, inc=1, device_id=(lax.rem(row + i, ROWS), col), device_id_type=mesh)

    lines[...] = jnp.zeros_like(lines)
    count_p, count_w = G_COL // LANES, G_ROW // LANES
    for i in range(count_p):
        lines[i : i + 1, :] = grid_map[pl.ds(col * count_p + i, 1), :].astype(jnp.float32)
    for i in range(count_w):
        lines[16 + i : 17 + i, :] = grid_map[pl.ds(row * count_w + i, 1), :].astype(jnp.float32)
    upright = jnp.transpose(lines[...], (1, 0)).astype(jnp.int32)
    for i in range(count_p):
        points_p[i * LANES : (i + 1) * LANES, :] = upright[:, i : i + 1]
    for i in range(count_w):
        points_w[i * LANES : (i + 1) * LANES, :] = upright[:, 16 + i : 17 + i]

    block = 4 * GRID
    first = lax.broadcasted_iota(jnp.int32, (block, LANES), 1) < GRID

    def widen(t, carry):
        slot_wave = cond[0, pl.ds(t * 4, 4)].reshape(block, LANES).astype(jnp.float32)
        turned = pltpu.roll(slot_wave, GRID, 1)
        slots[t, 0] = jnp.where(first, slot_wave, turned)
        slots[t, 1] = jnp.where(first, turned, slot_wave)
        return carry

    fetch_cond.wait()
    lax.fori_loop(0, GRID // 4, widen, 0, unroll=2)

    def transform(chunk, member):
        pair = 2 * chunk + member
        fetch_val[pair].wait()
        tb, ta, tc = table_b[...], table_a[...], table_c[...]

        def along_b(t, carry):
            rows = pl.ds(t * 4, 4)
            one = val[pair, 0, rows].reshape(block, LANES).astype(jnp.float32)
            two = val[pair, 1, rows].reshape(block, LANES).astype(jnp.float32)
            one_t = pltpu.roll(one, GRID, 1)
            two_t = pltpu.roll(two, GRID, 1)
            slot_re, slot_im = slots[t, 0], slots[t, 1]
            val_re = jnp.where(first, one, two_t)
            val_im = jnp.where(first, one_t, two)
            dens_re = val_re * slot_re + val_im * slot_im
            dens_im = val_re * slot_im - val_im * slot_re
            high, low = halves(jnp.concatenate([dens_re, dens_im], 1))
            both = three(dot_nn, tb, high, low)
            to = pl.ds(pl.multiple_of(t * 16, 16), 16)
            for sign, value in enumerate(signs(both, 4 * MAGS)):
                high, low = halves(value)
                for group in range(MAGS // 4):
                    zh[sign * 5 + group, to, :] = high[group * 16 : group * 16 + 16]
                    zl[sign * 5 + group, to, :] = low[group * 16 : group * 16 + 16]
            return carry

        lax.fori_loop(0, GRID // 4, along_b, 0, unroll=4)

        def along_a(group, carry):
            to = pl.ds(pl.multiple_of(group * 80, 16), 80)
            for sign_b in range(2):
                both = three(dot_nn, ta, zh[sign_b * 5 + group], zl[sign_b * 5 + group])
                for sign_a, value in enumerate(signs(both, 4 * MAGS)):
                    high, low = halves(value)
                    uh[sign_a * 2 + sign_b, to, :] = high
                    ul[sign_a * 2 + sign_b, to, :] = low
            return carry

        lax.fori_loop(0, MAGS // 4, along_a, 0, unroll=True)

        def along_c(quarter, carry):
            value = three(dot_nt, tc, uh[quarter], ul[quarter])
            value = value.reshape(MAGS, 8, CELLS)
            to = pl.multiple_of(quarter * 16 + member * 8, 8)
            sums[:, pl.ds(to, 8), :CELLS] = value
            sums[:, pl.ds(to + 64, 8), :CELLS] = value
            return carry

        lax.fori_loop(0, 4, along_c, 0, unroll=True)

    lane = lax.broadcasted_iota(jnp.int32, (1, LANES), 1)

    def collect(chunk):
        def upturn(mag, carry):
            value = jnp.transpose(sums[mag], (1, 0))
            cells[pl.ds(pl.multiple_of(mag * CELLS, 8), CELLS), :] = value[:CELLS]
            return carry

        lax.fori_loop(0, MAGS, upturn, 0, unroll=2)

        def gather(index, count):
            def rows(i, carry):
                for k in range(64):
                    at = i * 128 + 2 * k
                    even = cells[pl.ds(index[at], 1), :]
                    odd = cells[pl.ds(index[at + 1], 1), :]
                    picked[pl.ds(i * 64 + k, 1), :] = jnp.where(lane < 64, even, odd)
                return carry

            lax.fori_loop(0, count // 64, rows, 0)

        gather(index_p, plain.shape[1] * plain.shape[2])
        plain[chunk] = picked[...].astype(jnp.bfloat16).reshape(plain.shape[1:])
        count = weighted.shape[1] * weighted.shape[2]
        gather(index_w, count)
        band = (lane >> 3) % 2 * 2 + (lane >> 2) % 2
        gap = jnp.zeros((1, LANES), jnp.float32)
        energy = cond_energy[owner[0]]
        for v in range(4):
            gap = jnp.where(band == v, energy - val_energy[4 * chunk + v], gap)
        weight = -2.0 / (math.sqrt(8 * LANES) * gap)
        weighted[chunk] = (picked[:count] * weight).astype(jnp.bfloat16).reshape(weighted.shape[1:])

    def push(src, dst, send, recv, device):
        return pltpu.make_async_remote_copy(
            src_ref=src, dst_ref=dst, send_sem=send, recv_sem=recv, device_id=device, device_id_type=mesh
        )

    sent = []
    row_copies, col_copies, own_copies = {}, {}, {}

    def swap(chunk):
        copies = []
        for i in range(1, ROWS):
            to, at = lax.rem(row + i, ROWS), chunk * ROWS + i
            copy = push(
                weighted.at[chunk].at[to], slabs_w.at[chunk].at[row], row_send.at[at], row_recv.at[at], (to, col)
            )
            copy.start()
            copies.append(copy)
        row_copies[chunk] = copies
        copies = []
        for i in range(1, COLS):
            to, at = lax.rem(col + i, COLS), chunk * COLS + i
            copy = push(
                plain.at[chunk].at[to], slabs.at[chunk].at[slot], col_send.at[at], col_recv.at[at], (row, to)
            )
            copy.start()
            copies.append(copy)
        col_copies[chunk] = copies
        own_p = pltpu.make_async_copy(plain.at[chunk].at[col], slabs.at[chunk].at[slot], own_sem.at[2 * chunk])
        own_w = pltpu.make_async_copy(
            weighted.at[chunk].at[row], slabs_w.at[chunk].at[row], own_sem.at[2 * chunk + 1]
        )
        own_p.start()
        own_w.start()
        own_copies[chunk] = own_p, own_w
        sent.extend(row_copies[chunk] + col_copies[chunk])

    beside, spread, twin = {}, {}, {}

    def place_left(chunk):
        own_copies[chunk][1].wait()
        for copy in row_copies[chunk]:
            copy.wait_recv()
        value = placed(
            points_w[...], codes_w[row], [slabs_w[chunk, i] for i in range(ROWS)], fold_w[...]
        )
        lefts[chunk, slot] = jnp.transpose(value, (1, 0))[:64].astype(jnp.bfloat16)
        mine = lefts.at[chunk].at[slot]
        beside[chunk] = push(
            mine, mine, left_send.at[chunk * 5], left_recv.at[chunk * 5],
            (row, (x * 2 + 1 - y_lo) * 2 + core),
        )
        beside[chunk].start()
        sent.append(beside[chunk])

    def spread_left(chunk):
        beside[chunk].wait_recv()
        spread[chunk] = []
        two = lefts.at[chunk].at[pl.ds(core * 8 + x * 2, 2)]
        for i in range(1, 4):
            to, at = lax.rem(x + i, 4), chunk * 5 + i
            copy = push(two, two, left_send.at[at], left_recv.at[at], (row, (to * 2 + y_lo) * 2 + core))
            copy.start()
            spread[chunk].append(copy)
        sent.extend(spread[chunk])

    def twin_left(chunk):
        for copy in spread[chunk]:
            copy.wait_recv()
        octet, at = lefts.at[chunk].at[pl.ds(core * 8, 8)], chunk * 5 + 4
        twin[chunk] = push(octet, octet, left_send.at[at], left_recv.at[at], (row, col + 1 - 2 * core))
        twin[chunk].start()
        sent.append(twin[chunk])

    def build_left(chunk):
        twin[chunk].wait_recv()
        lefts_wide[...] = lefts[chunk].astype(jnp.float32)
        for source in range(ROWS):
            value = lefts_wide[:, source * 8 : source * 8 + 8, :].reshape(LANES, G_ROW)
            value = jnp.transpose(value, (1, 0)).astype(jnp.bfloat16)
            lanes = slice(source * LANES, (source + 1) * LANES)
            left[chunk, :G_ROW, lanes] = value
            left[chunk, G_ROW:, lanes] = dot_nn(value, turn[...]).astype(jnp.bfloat16)

    moves = {}

    def move(chunk, tile, kind, source, device, half=None):
        if half is None:
            rows = pl.ds(tile * TILE, TILE)
        else:
            rows = pl.ds(tile * TILE + half * (TILE // 2), TILE // 2)
        part = panels.at[chunk].at[source].at[rows]
        at = (chunk * TILES + tile) * KINDS + kind
        copy = push(part, part, move_send.at[at], move_recv.at[at], device)
        copy.start()
        moves[chunk, tile, kind] = copy
        sent.append(copy)

    starts, span = windows(G_COL, COLS, TILE)

    def place(chunk):
        own_copies[chunk][0].wait()
        for copy in col_copies[chunk]:
            copy.wait_recv()
        for tile in range(TILES):
            window = slice(starts[tile], starts[tile] + span)
            value = placed(
                points_p[tile * TILE : (tile + 1) * TILE], codes_p[col][:, window],
                [slabs[chunk, i, window] for i in range(COLS)], fold_p[...],
            )
            panels[chunk, row, tile * TILE : (tile + 1) * TILE, :] = value.astype(jnp.bfloat16)
            move(chunk, tile, 0, row, across)
            move(chunk, tile, 1, row, above)
            move(chunk, tile, 2, row, below)

    y_first, z_first = range(3), range(3, TILES)

    def pass_on(chunk, tile, y, kinds):
        moves[chunk, tile, kinds[0]].wait_recv()
        move(chunk, tile, kinds[2], down * 2 + y, above, 0)
        moves[chunk, tile, kinds[1]].wait_recv()
        move(chunk, tile, kinds[3], up * 2 + y, below, 1)

    def wave_one(chunk):
        for tile in y_first:
            moves[chunk, tile, 0].wait_recv()
            move(chunk, tile, 5, across_row, above)
            move(chunk, tile, 6, across_row, below)
            pass_on(chunk, tile, y_hi, (1, 2, 3, 4))

    def wave_two(chunk):
        for tile in z_first:
            pass_on(chunk, tile, y_hi, (1, 2, 3, 4))
            move(chunk, tile, 5, down * 2 + y_hi, across)
            move(chunk, tile, 6, up * 2 + y_hi, across)
        for tile in y_first:
            pass_on(chunk, tile, 1 - y_hi, (5, 6, 7, 8))

    def wave_three(chunk):
        for tile in z_first:
            moves[chunk, tile, 3].wait_recv()
            move(chunk, tile, 7, far * 2 + y_hi, across, 0)
            moves[chunk, tile, 4].wait_recv()
            move(chunk, tile, 8, far * 2 + y_hi, across, 1)

    outs = []

    def multiply(chunk, tile):
        for kind in (3, 4, 7, 8) if tile in y_first else (0, 5, 6, 7, 8):
            moves[chunk, tile, kind].wait_recv()
        rows = slice(tile * TILE, (tile + 1) * TILE)
        right = jnp.concatenate([panels[chunk, source, rows, :] for source in range(ROWS)], 1)
        value = dot_nt(left[chunk], right).reshape(2, G_ROW, TILE)
        if chunk == 0:
            totals[tile] = value
            return
        totals[tile] = totals[tile] + value
        copy = pltpu.make_async_copy(
            totals.at[tile], out.at[:, :, pl.ds(tile * TILE, TILE)], out_sem.at[tile]
        )
        copy.start()
        outs.append(copy)

    transform(0, 0)
    transform(0, 1)
    collect(0)
    pl.semaphore_wait(barrier, COLS + ROWS - 2)
    swap(0)
    transform(1, 0)
    place_left(0)
    place(0)
    transform(1, 1)
    wave_one(0)
    spread_left(0)
    collect(1)
    swap(1)
    wave_two(0)
    twin_left(0)
    place_left(1)
    place(1)
    wave_three(0)
    spread_left(1)
    wave_one(1)
    build_left(0)
    for tile in range(3):
        multiply(0, tile)
    twin_left(1)
    wave_two(1)
    for tile in range(3, TILES):
        multiply(0, tile)
    wave_three(1)
    build_left(1)
    for tile in range(TILES):
        multiply(1, tile)
    for copy in sent:
        copy.wait_send()
    for copy in outs:
        copy.wait()


def on_device(val_wave, cond_wave, val_energy, cond_energy, band_owner, grid_map):
    index_p, codes_p, _ = orbit_lists(G_COL, COLS)
    index_w, codes_w, _ = orbit_lists(G_ROW, ROWS)
    codes_p, codes_w = paired(codes_p), paired(codes_w)
    rows_p, rows_w = codes_p.shape[2], codes_w.shape[2]
    constants = [
        codes_p, codes_w, *dft_tables(),
        fold_table(COLS, LANES), fold_table(ROWS, LANES), turn_table(),
    ]
    smem = pl.BlockSpec(memory_space=pltpu.SMEM)
    vmem = pl.BlockSpec(memory_space=pltpu.VMEM)
    hbm = pl.BlockSpec(memory_space=pl.ANY)
    dma = pltpu.SemaphoreType.DMA
    bf16, f32 = jnp.bfloat16, jnp.float32
    return pl.pallas_call(
        whole_kernel,
        in_specs=[smem] * 5 + [vmem] * (1 + len(constants)) + [hbm] * 2,
        out_specs=hbm,
        out_shape=jax.ShapeDtypeStruct((2, G_ROW, G_COL), f32),
        scratch_shapes=[
            pltpu.VMEM((4, 2, GRID, GRID, LANES), bf16),
            pltpu.VMEM((1, GRID, GRID, LANES), bf16),
            pltpu.VMEM((GRID // 4, 2, 4 * GRID, LANES), f32),
            pltpu.VMEM((10, 4 * GRID, 2 * LANES), bf16),
            pltpu.VMEM((10, 4 * GRID, 2 * LANES), bf16),
            pltpu.VMEM((4, CELLS, 2 * LANES), bf16),
            pltpu.VMEM((4, CELLS, 2 * LANES), bf16),
            pltpu.VMEM((MAGS, LANES, 512), f32),
            pltpu.VMEM((MAGS * CELLS, LANES), f32),
            pltpu.VMEM((COLS * rows_p, LANES), f32),
            pltpu.VMEM((G_COL, 1), jnp.int32),
            pltpu.VMEM((G_ROW, 1), jnp.int32),
            pltpu.VMEM((LANES, LANES), f32),
            pltpu.VMEM((2, COLS, rows_p, LANES), bf16),
            pltpu.VMEM((2, ROWS, rows_w, LANES), bf16),
            pltpu.VMEM((2, COLS, rows_p, LANES), bf16),
            pltpu.VMEM((2, ROWS, rows_w, LANES), bf16),
            pltpu.VMEM((2, COLS, 64, G_ROW), bf16),
            pltpu.VMEM((COLS, 64, G_ROW), f32),
            pltpu.VMEM((2, 2 * G_ROW, ROWS * LANES), bf16),
            pltpu.VMEM((2, ROWS, G_COL, LANES), bf16),
            pltpu.VMEM((TILES, 2, G_ROW, TILE), f32),
            dma((4,)), dma, dma((4,)), dma((TILES,)),
            dma((2 * COLS,)), dma((2 * COLS,)), dma((2 * ROWS,)), dma((2 * ROWS,)), dma((10,)), dma((10,)),
            dma((2 * TILES * KINDS,)), dma((2 * TILES * KINDS,)),
        ],
        compiler_params=pltpu.CompilerParams(
            collective_id=0, has_side_effects=True, vmem_limit_bytes=62 * 2**20
        ),
        name="whole",
    )(
        band_owner, cond_energy, val_energy, jnp.asarray(index_p.ravel()), jnp.asarray(index_w.ravel()),
        grid_map.reshape(NG // LANES, LANES), *(jnp.asarray(value) for value in constants),
        val_wave, cond_wave,
    )


def solution(mesh):
    in_specs = (P(), P(("row", "col"), None, None, None), P(), P(), P(("row", "col")), P())
    out_specs = P(None, "row", "col")
    return jax.shard_map(
        on_device, mesh=mesh, in_specs=in_specs, out_specs=out_specs, check_vma=False
    )
```

```python
import math

import jax
import jax.numpy as jnp
import ml_dtypes
import numpy as np
from jax import lax
from jax.experimental import pallas as pl
from jax.experimental.pallas import tpu as pltpu
from jax.sharding import PartitionSpec as P

GRID = 64
NG = 30720
SLAB = 2048
ROWS = 8
COLS = 16
G_COL = NG // COLS
G_ROW = SLAB // ROWS
MAGS = 20
CELLS = MAGS * MAGS
LANES = 128


def shells():
    points = np.arange(GRID)
    freq = np.where(points < GRID // 2, points, points - GRID)
    square = freq * freq
    length = (square[:, None, None] + square[None, :, None] + square[None, None, :]).ravel()
    length = np.sort(length, kind="stable")
    assert length[NG - 1] < MAGS * MAGS
    return length


def orbit_lists(width, count):
    length = shells()
    mags = np.arange(MAGS)
    a, b, c = np.meshgrid(mags, mags, mags, indexing="ij")
    a, b, c = a.ravel(), b.ravel(), c.ravel()
    square = a * a + b * b + c * c
    source = c * CELLS + (b // 4) * (4 * MAGS) + a * 4 + b % 4
    code = (a * GRID + b) * GRID + c
    order = np.argsort(square, kind="stable")
    lists = []
    for block in range(count):
        least, most = length[block * width], length[(block + 1) * width - 1]
        lists.append(order[(square[order] >= least) & (square[order] <= most)])
    rows = -(-max(len(picked) for picked in lists) // 16) * 16
    index = np.zeros((count, rows), np.int32)
    codes = np.full((count, 1, rows), -1, np.int32)
    for block, picked in enumerate(lists):
        index[block, : len(picked)] = source[picked]
        codes[block, 0, : len(picked)] = code[picked]
    return index, codes, [square[picked] for picked in lists]


def split_table(table):
    high = table.astype(ml_dtypes.bfloat16)
    low = (table - high.astype(np.float64)).astype(ml_dtypes.bfloat16)
    return np.concatenate([high, low], 0)


def dft_tables():
    point = np.arange(GRID)
    mag = np.arange(MAGS)
    angle = (mag[:, None] * point[None, :] % GRID) * (2.0 * math.pi / GRID)
    parts = np.stack([np.cos(angle), np.sin(angle)])
    table_b = np.zeros((2, MAGS // 4, 4, 4, 4, GRID))
    for a in range(4):
        table_b[:, :, a, :, a, :] = parts.reshape(2, MAGS // 4, 4, GRID)
    table_a = np.zeros((2, MAGS, 4, GRID, 4))
    for b in range(4):
        table_a[:, :, b, :, b] = parts
    table_c = np.zeros((MAGS, 2, 2, 2, 2, 2, GRID))
    for v in range(2):
        for sign in range(2):
            turn = 1.0 - 2.0 * sign
            table_c[:, v, 0, sign, 0, v] = parts[0]
            table_c[:, v, 0, sign, 1, v] = turn * parts[1]
            table_c[:, v, 1, sign, 1, v] = parts[0]
            table_c[:, v, 1, sign, 0, v] = -turn * parts[1]
    table_c = table_c * (1.0 / float(GRID) ** 1.5)
    return (
        split_table(table_b.reshape(8 * MAGS, 4 * GRID)),
        split_table(table_a.reshape(8 * MAGS, 4 * GRID)),
        split_table(table_c.reshape(8 * MAGS, 4 * GRID)),
    )


def dot_nn(left, right):
    return lax.dot_general(
        left, right, (((1,), (0,)), ((), ())), preferred_element_type=jnp.float32
    )


def dot_nt(left, right):
    return lax.dot_general(
        left, right, (((1,), (1,)), ((), ())), preferred_element_type=jnp.float32
    )


def halves(value):
    high = value.astype(jnp.bfloat16)
    return high, (value - high.astype(jnp.float32)).astype(jnp.bfloat16)


def three(dot, table, high, low):
    rows = table.shape[0] // 2
    both = dot(table, high)
    return both[:rows] + both[rows:] + dot(table[:rows], low)


def signs(both, rows):
    cos_re, cos_im = both[:rows, :LANES], both[:rows, LANES:]
    sin_re, sin_im = both[rows:, :LANES], both[rows:, LANES:]
    plus = jnp.concatenate([cos_re + sin_im, cos_im - sin_re], 1)
    minus = jnp.concatenate([cos_re - sin_im, cos_im + sin_re], 1)
    return plus, minus


def windows(width, count, tile):
    length = shells()
    _, codes, squares = orbit_lists(width, count)
    starts, ends = [], []
    for at in range(0, width, tile):
        first, last = [], []
        for block, square in enumerate(squares):
            first.append(np.searchsorted(square, length[block * width + at], "left"))
            last.append(np.searchsorted(square, length[block * width + at + tile - 1], "right"))
        starts.append(int(min(first)) // 32 * 16)
        ends.append(-(-int(max(last)) // 2))
    rows = max(-(-(end - start) // 16) * 16 for start, end in zip(starts, ends))
    return [min(start, codes.shape[2] // 2 - rows) for start in starts], rows


def paired(codes):
    return np.stack([codes[:, 0, 0::2], codes[:, 0, 1::2]], 1)


def fold_table(count, width):
    fold = np.zeros((count, LANES, width), ml_dtypes.bfloat16)
    lane = np.arange(LANES)
    for source in range(count):
        fold[source, lane, source * 8 + (lane >> 1) % 8] = 1.0
    return fold.reshape(count * LANES, width)


def turn_table():
    table = np.zeros((LANES, LANES), ml_dtypes.bfloat16)
    lane = np.arange(0, LANES, 2)
    table[lane + 1, lane] = 1.0
    table[lane, lane + 1] = -1.0
    return table


def placed(point, codes, slabs, fold):
    a, b, c = point >> 12, (point >> 6) & 63, point & 63
    half = GRID // 2
    code = (jnp.where(a > half, GRID - a, a) * GRID + jnp.where(b > half, GRID - b, b)) * GRID
    code = code + jnp.where(c > half, GRID - c, c)
    odd = jnp.where(code == codes[1:2], 1.0, 0.0)
    hot = jnp.where(code == codes[0:1], 1.0, odd).astype(jnp.bfloat16)
    key = (
        jnp.where(jnp.sum(odd, axis=1, keepdims=True) > 0.5, 8, 0)
        + jnp.where(a > half, 4, 0) + jnp.where(b > half, 2, 0) + jnp.where(c > half, 1, 0)
    )
    lane = lax.broadcasted_iota(jnp.int32, (1, 2 * LANES), 1) % LANES
    own = key == (lane >> 4) * 2 + lane % 2
    rows = []
    for pair in range(len(slabs) // 2):
        both = jnp.concatenate([slabs[2 * pair], slabs[2 * pair + 1]], 1)
        rows.append(jnp.where(own, dot_nn(hot, both), 0.0).astype(jnp.bfloat16))
    return dot_nn(jnp.concatenate(rows, 1), fold)


TILE = 384
TILES = G_COL // TILE
KINDS = 9


def whole_kernel(
    owner, cond_energy, val_energy, index_p, index_w,
    grid_map, codes_p, codes_w, table_b, table_a, table_c, fold_p, fold_w, turn, val_hbm, cond_hbm,
    out,
    val, cond, slots, zh, zl, uh, ul, sums, cells, picked, points_p, points_w, lines,
    plain, weighted, slabs, slabs_w, lefts, lefts_wide, left, panels, totals,
    val_sem, cond_sem, own_sem, out_sem,
    col_send, col_recv, row_send, row_recv, left_send, left_recv, move_send, move_recv,
):
    row, col = lax.axis_index("row"), lax.axis_index("col")
    z, y_hi = row // 2, lax.rem(row, 2)
    x, y_lo, core = col // 4, lax.rem(col // 2, 2), lax.rem(col, 2)
    up, down, far = lax.rem(z + 1, 4), lax.rem(z + 3, 4), lax.rem(z + 2, 4)
    above, below = (up * 2 + y_hi, col), (down * 2 + y_hi, col)
    across_row = z * 2 + 1 - y_hi
    across = (across_row, col)
    slot = core * 8 + col // 2
    mesh = pl.DeviceIdType.MESH

    fetch_cond = pltpu.make_async_copy(cond_hbm, cond, cond_sem)
    fetch_cond.start()
    fetch_val = []
    for pair in range(4):
        copy = pltpu.make_async_copy(val_hbm.at[pl.ds(2 * pair, 2)], val.at[pair], val_sem.at[pair])
        copy.start()
        fetch_val.append(copy)

    barrier = pltpu.get_barrier_semaphore()
    for i in range(1, COLS):
        pl.semaphore_signal(barrier, inc=1, device_id=(row, lax.rem(col + i, COLS)), device_id_type=mesh)
    for i in range(1, ROWS):
        pl.semaphore_signal(barrier, inc=1, device_id=(lax.rem(row + i, ROWS), col), device_id_type=mesh)

    lines[...] = jnp.zeros_like(lines)
    count_p, count_w = G_COL // LANES, G_ROW // LANES
    for i in range(count_p):
        lines[i : i + 1, :] = grid_map[pl.ds(col * count_p + i, 1), :].astype(jnp.float32)
    for i in range(count_w):
        lines[16 + i : 17 + i, :] = grid_map[pl.ds(row * count_w + i, 1), :].astype(jnp.float32)
    upright = jnp.transpose(lines[...], (1, 0)).astype(jnp.int32)
    for i in range(count_p):
        points_p[i * LANES : (i + 1) * LANES, :] = upright[:, i : i + 1]
    for i in range(count_w):
        points_w[i * LANES : (i + 1) * LANES, :] = upright[:, 16 + i : 17 + i]

    block = 4 * GRID
    first = lax.broadcasted_iota(jnp.int32, (block, LANES), 1) < GRID

    def widen(t, carry):
        slot_wave = cond[0, pl.ds(t * 4, 4)].reshape(block, LANES).astype(jnp.float32)
        turned = pltpu.roll(slot_wave, GRID, 1)
        slots[t, 0] = jnp.where(first, slot_wave, turned)
        slots[t, 1] = jnp.where(first, turned, slot_wave)
        return carry

    fetch_cond.wait()
    lax.fori_loop(0, GRID // 4, widen, 0, unroll=2)

    def transform_b(chunk, member):
        pair = 2 * chunk + member
        fetch_val[pair].wait()
        tb = table_b[...]

        def along_b(t, carry):
            rows = pl.ds(t * 4, 4)
            one = val[pair, 0, rows].reshape(block, LANES).astype(jnp.float32)
            two = val[pair, 1, rows].reshape(block, LANES).astype(jnp.float32)
            one_t = pltpu.roll(one, GRID, 1)
            two_t = pltpu.roll(two, GRID, 1)
            slot_re, slot_im = slots[t, 0], slots[t, 1]
            val_re = jnp.where(first, one, two_t)
            val_im = jnp.where(first, one_t, two)
            dens_re = val_re * slot_re + val_im * slot_im
            dens_im = val_re * slot_im - val_im * slot_re
            high, low = halves(jnp.concatenate([dens_re, dens_im], 1))
            both = three(dot_nn, tb, high, low)
            to = pl.ds(pl.multiple_of(t * 16, 16), 16)
            for sign, value in enumerate(signs(both, 4 * MAGS)):
                high, low = halves(value)
                for group in range(MAGS // 4):
                    zh[sign * 5 + group, to, :] = high[group * 16 : group * 16 + 16]
                    zl[sign * 5 + group, to, :] = low[group * 16 : group * 16 + 16]
            return carry

        lax.fori_loop(0, GRID // 4, along_b, 0, unroll=8)

    def transform_ac(member):
        ta, tc = table_a[...], table_c[...]

        def along_a(group, carry):
            to = pl.ds(pl.multiple_of(group * 80, 16), 80)
            for sign_b in range(2):
                both = three(dot_nn, ta, zh[sign_b * 5 + group], zl[sign_b * 5 + group])
                for sign_a, value in enumerate(signs(both, 4 * MAGS)):
                    high, low = halves(value)
                    uh[sign_a * 2 + sign_b, to, :] = high
                    ul[sign_a * 2 + sign_b, to, :] = low
            return carry

        lax.fori_loop(0, MAGS // 4, along_a, 0, unroll=True)

        def along_c(quarter, carry):
            value = three(dot_nt, tc, uh[quarter], ul[quarter])
            value = value.reshape(MAGS, 8, CELLS)
            to = pl.multiple_of(quarter * 16 + member * 8, 8)
            sums[:, pl.ds(to, 8), :CELLS] = value
            sums[:, pl.ds(to + 64, 8), :CELLS] = value
            return carry

        lax.fori_loop(0, 4, along_c, 0, unroll=True)

    lane = lax.broadcasted_iota(jnp.int32, (1, LANES), 1)

    def collect():
        def upturn(mag, carry):
            value = jnp.transpose(sums[mag], (1, 0))
            cells[pl.ds(pl.multiple_of(mag * CELLS, 8), CELLS), :] = value[:CELLS]
            return carry

        lax.fori_loop(0, MAGS, upturn, 0, unroll=2)

    def gather(index, base, to, count):
        def rows(i, carry):
            for k in range(32):
                at = base + i * 64 + 2 * k
                even = cells[pl.ds(index[at], 1), :]
                odd = cells[pl.ds(index[at + 1], 1), :]
                picked[pl.ds(to + i * 32 + k, 1), :] = jnp.where(lane < 64, even, odd)
            return carry

        lax.fori_loop(0, count // 32, rows, 0)

    def push(src, dst, send, recv, device):
        return pltpu.make_async_remote_copy(
            src_ref=src, dst_ref=dst, send_sem=send, recv_sem=recv, device_id=device, device_id_type=mesh
        )

    sent = []
    row_copies, col_copies, own_copies = {}, {}, {}

    def swap(chunk):
        rows = plain.shape[2]
        copies = []
        for i in list(range(1, COLS)) + [0]:
            to, at = lax.rem(col + i, COLS), chunk * COLS + i
            gather(index_p, to * (2 * rows), i * rows, rows)
            plain[chunk, to] = picked[i * rows : (i + 1) * rows].astype(jnp.bfloat16)
            src, dst = plain.at[chunk].at[to], slabs.at[chunk].at[slot]
            if i == 0:
                own_p = pltpu.make_async_copy(src, dst, own_sem.at[2 * chunk])
                own_p.start()
            else:
                copy = push(src, dst, col_send.at[at], col_recv.at[at], (row, to))
                copy.start()
                copies.append(copy)
        col_copies[chunk] = copies
        count = weighted.shape[1] * weighted.shape[2]
        gather(index_w, 0, 0, count)
        band = (lane >> 3) % 2 * 2 + (lane >> 2) % 2
        gap = jnp.zeros((1, LANES), jnp.float32)
        energy = cond_energy[owner[0]]
        for v in range(4):
            gap = jnp.where(band == v, energy - val_energy[4 * chunk + v], gap)
        weight = -2.0 / (math.sqrt(8 * LANES) * gap)
        weighted[chunk] = (picked[:count] * weight).astype(jnp.bfloat16).reshape(weighted.shape[1:])
        copies = []
        for i in range(1, ROWS):
            to, at = lax.rem(row + i, ROWS), chunk * ROWS + i
            copy = push(
                weighted.at[chunk].at[to], slabs_w.at[chunk].at[row], row_send.at[at], row_recv.at[at], (to, col)
            )
            copy.start()
            copies.append(copy)
        row_copies[chunk] = copies
        own_w = pltpu.make_async_copy(
            weighted.at[chunk].at[row], slabs_w.at[chunk].at[row], own_sem.at[2 * chunk + 1]
        )
        own_w.start()
        own_copies[chunk] = own_p, own_w
        sent.extend(row_copies[chunk] + col_copies[chunk])

    beside, spread, twin = {}, {}, {}

    def place_left(chunk):
        own_copies[chunk][1].wait()
        for copy in row_copies[chunk]:
            copy.wait_recv()
        value = placed(
            points_w[...], codes_w[row], [slabs_w[chunk, i] for i in range(ROWS)], fold_w[...]
        )
        lefts[chunk, slot] = jnp.transpose(value, (1, 0))[:64].astype(jnp.bfloat16)
        mine = lefts.at[chunk].at[slot]
        beside[chunk] = push(
            mine, mine, left_send.at[chunk * 5], left_recv.at[chunk * 5],
            (row, (x * 2 + 1 - y_lo) * 2 + core),
        )
        beside[chunk].start()
        sent.append(beside[chunk])

    def spread_left(chunk):
        beside[chunk].wait_recv()
        spread[chunk] = []
        two = lefts.at[chunk].at[pl.ds(core * 8 + x * 2, 2)]
        for i in range(1, 4):
            to, at = lax.rem(x + i, 4), chunk * 5 + i
            copy = push(two, two, left_send.at[at], left_recv.at[at], (row, (to * 2 + y_lo) * 2 + core))
            copy.start()
            spread[chunk].append(copy)
        sent.extend(spread[chunk])

    def twin_left(chunk):
        for copy in spread[chunk]:
            copy.wait_recv()
        octet, at = lefts.at[chunk].at[pl.ds(core * 8, 8)], chunk * 5 + 4
        twin[chunk] = push(octet, octet, left_send.at[at], left_recv.at[at], (row, col + 1 - 2 * core))
        twin[chunk].start()
        sent.append(twin[chunk])

    def build_left(chunk):
        twin[chunk].wait_recv()
        lefts_wide[...] = lefts[chunk].astype(jnp.float32)
        for source in range(ROWS):
            value = lefts_wide[:, source * 8 : source * 8 + 8, :].reshape(LANES, G_ROW)
            value = jnp.transpose(value, (1, 0)).astype(jnp.bfloat16)
            lanes = slice(source * LANES, (source + 1) * LANES)
            left[chunk, :G_ROW, lanes] = value
            left[chunk, G_ROW:, lanes] = dot_nn(value, turn[...]).astype(jnp.bfloat16)

    moves = {}

    def move(chunk, tile, kind, source, device, half=None):
        if half is None:
            rows = pl.ds(tile * TILE, TILE)
        else:
            rows = pl.ds(tile * TILE + half * (TILE // 2), TILE // 2)
        part = panels.at[chunk].at[source].at[rows]
        at = (chunk * TILES + tile) * KINDS + kind
        copy = push(part, part, move_send.at[at], move_recv.at[at], device)
        copy.start()
        moves[chunk, tile, kind] = copy
        sent.append(copy)

    starts, span = windows(G_COL, COLS, TILE)

    def place(chunk):
        own_copies[chunk][0].wait()
        for copy in col_copies[chunk]:
            copy.wait_recv()
        for tile in range(TILES):
            window = slice(starts[tile], starts[tile] + span)
            value = placed(
                points_p[tile * TILE : (tile + 1) * TILE], codes_p[col][:, window],
                [slabs[chunk, i, window] for i in range(COLS)], fold_p[...],
            )
            panels[chunk, row, tile * TILE : (tile + 1) * TILE, :] = value.astype(jnp.bfloat16)
            move(chunk, tile, 0, row, across)
            move(chunk, tile, 1, row, above)
            move(chunk, tile, 2, row, below)

    y_first, z_first = range(3), range(3, TILES)

    def pass_on(chunk, tile, y, kinds):
        moves[chunk, tile, kinds[0]].wait_recv()
        move(chunk, tile, kinds[2], down * 2 + y, above, 0)
        moves[chunk, tile, kinds[1]].wait_recv()
        move(chunk, tile, kinds[3], up * 2 + y, below, 1)

    def wave_one(chunk):
        for tile in y_first:
            moves[chunk, tile, 0].wait_recv()
            move(chunk, tile, 5, across_row, above)
            move(chunk, tile, 6, across_row, below)
            pass_on(chunk, tile, y_hi, (1, 2, 3, 4))

    def wave_two(chunk):
        for tile in z_first:
            pass_on(chunk, tile, y_hi, (1, 2, 3, 4))
            move(chunk, tile, 5, down * 2 + y_hi, across)
            move(chunk, tile, 6, up * 2 + y_hi, across)
        for tile in y_first:
            pass_on(chunk, tile, 1 - y_hi, (5, 6, 7, 8))

    def wave_three(chunk):
        for tile in z_first:
            moves[chunk, tile, 3].wait_recv()
            move(chunk, tile, 7, far * 2 + y_hi, across, 0)
            moves[chunk, tile, 4].wait_recv()
            move(chunk, tile, 8, far * 2 + y_hi, across, 1)

    outs = []

    def multiply(chunk, tile):
        for kind in (3, 4, 7, 8) if tile in y_first else (0, 5, 6, 7, 8):
            moves[chunk, tile, kind].wait_recv()
        rows = slice(tile * TILE, (tile + 1) * TILE)
        right = jnp.concatenate([panels[chunk, source, rows, :] for source in range(ROWS)], 1)
        value = dot_nt(left[chunk], right).reshape(2, G_ROW, TILE)
        if chunk == 0:
            totals[tile] = value
            return
        totals[tile] = totals[tile] + value
        copy = pltpu.make_async_copy(
            totals.at[tile], out.at[:, :, pl.ds(tile * TILE, TILE)], out_sem.at[tile]
        )
        copy.start()
        outs.append(copy)

    for member in range(2):
        transform_b(0, member)
        transform_ac(member)
    collect()
    pl.semaphore_wait(barrier, COLS + ROWS - 2)
    swap(0)
    transform_b(1, 0)
    transform_ac(0)
    transform_b(1, 1)
    place(0)
    transform_ac(1)
    collect()
    swap(1)
    wave_one(0)
    place_left(0)
    wave_two(0)
    spread_left(0)
    place(1)
    wave_three(0)
    twin_left(0)
    place_left(1)
    wave_one(1)
    build_left(0)
    for tile in range(3):
        multiply(0, tile)
    spread_left(1)
    wave_two(1)
    twin_left(1)
    for tile in range(3, TILES):
        multiply(0, tile)
    wave_three(1)
    build_left(1)
    for tile in range(TILES):
        multiply(1, tile)
    for copy in sent:
        copy.wait_send()
    for copy in outs:
        copy.wait()


def on_device(val_wave, cond_wave, val_energy, cond_energy, band_owner, grid_map):
    index_p, codes_p, _ = orbit_lists(G_COL, COLS)
    index_w, codes_w, _ = orbit_lists(G_ROW, ROWS)
    codes_p, codes_w = paired(codes_p), paired(codes_w)
    rows_p, rows_w = codes_p.shape[2], codes_w.shape[2]
    constants = [
        codes_p, codes_w, *dft_tables(),
        fold_table(COLS, LANES), fold_table(ROWS, LANES), turn_table(),
    ]
    smem = pl.BlockSpec(memory_space=pltpu.SMEM)
    vmem = pl.BlockSpec(memory_space=pltpu.VMEM)
    hbm = pl.BlockSpec(memory_space=pl.ANY)
    dma = pltpu.SemaphoreType.DMA
    bf16, f32 = jnp.bfloat16, jnp.float32
    return pl.pallas_call(
        whole_kernel,
        in_specs=[smem] * 5 + [vmem] * (1 + len(constants)) + [hbm] * 2,
        out_specs=hbm,
        out_shape=jax.ShapeDtypeStruct((2, G_ROW, G_COL), f32),
        scratch_shapes=[
            pltpu.VMEM((4, 2, GRID, GRID, LANES), bf16),
            pltpu.VMEM((1, GRID, GRID, LANES), bf16),
            pltpu.VMEM((GRID // 4, 2, 4 * GRID, LANES), f32),
            pltpu.VMEM((10, 4 * GRID, 2 * LANES), bf16),
            pltpu.VMEM((10, 4 * GRID, 2 * LANES), bf16),
            pltpu.VMEM((4, CELLS, 2 * LANES), bf16),
            pltpu.VMEM((4, CELLS, 2 * LANES), bf16),
            pltpu.VMEM((MAGS, LANES, 512), f32),
            pltpu.VMEM((MAGS * CELLS, LANES), f32),
            pltpu.VMEM((COLS * rows_p, LANES), f32),
            pltpu.VMEM((G_COL, 1), jnp.int32),
            pltpu.VMEM((G_ROW, 1), jnp.int32),
            pltpu.VMEM((LANES, LANES), f32),
            pltpu.VMEM((2, COLS, rows_p, LANES), bf16),
            pltpu.VMEM((2, ROWS, rows_w, LANES), bf16),
            pltpu.VMEM((2, COLS, rows_p, LANES), bf16),
            pltpu.VMEM((2, ROWS, rows_w, LANES), bf16),
            pltpu.VMEM((2, COLS, 64, G_ROW), bf16),
            pltpu.VMEM((COLS, 64, G_ROW), f32),
            pltpu.VMEM((2, 2 * G_ROW, ROWS * LANES), bf16),
            pltpu.VMEM((2, ROWS, G_COL, LANES), bf16),
            pltpu.VMEM((TILES, 2, G_ROW, TILE), f32),
            dma((4,)), dma, dma((4,)), dma((TILES,)),
            dma((2 * COLS,)), dma((2 * COLS,)), dma((2 * ROWS,)), dma((2 * ROWS,)), dma((10,)), dma((10,)),
            dma((2 * TILES * KINDS,)), dma((2 * TILES * KINDS,)),
        ],
        compiler_params=pltpu.CompilerParams(
            collective_id=0, has_side_effects=True, vmem_limit_bytes=62 * 2**20
        ),
        name="whole",
    )(
        band_owner, cond_energy, val_energy, jnp.asarray(index_p.ravel()), jnp.asarray(index_w.ravel()),
        grid_map.reshape(NG // LANES, LANES), *(jnp.asarray(value) for value in constants),
        val_wave, cond_wave,
    )


def solution(mesh):
    in_specs = (P(), P(("row", "col"), None, None, None), P(), P(), P(("row", "col")), P())
    out_specs = P(None, "row", "col")
    return jax.shard_map(
        on_device, mesh=mesh, in_specs=in_specs, out_specs=out_specs, check_vma=False
    )
```
